768 devices in a mesh: freq: 32 (over x, y), rcv: 24 (over z, core).
Axes of the slice: x: 4, y: 8, z: 12, core: 2. Of those that a mesh axis runs over, the one named last changes fastest.
Arguments:
- traces: bfloat16 [64, 3072, 1024], P('freq', 'rcv'), may hold values from -6 to 6
- kern_v: bfloat16 [128, 3072, 12, 128], P('freq', 'rcv'), may hold values from -0.375 to 0.375
- kern_u: bfloat16 [128, 24, 1536, 128], P('freq', 'rcv'), may hold values from -0.15625 to 0.15625
- assign: int32 [128], replicated, may hold values from 0 to 127, each once
- tile_rank: int32 [128, 12, 24], P('freq', None, 'rcv'), may hold values from 4 to 64, as said below
Outputs:
- redatumed: float32 [1536, 64, 1024], P('rcv', 'freq')
The draws below stay inside these ranges and needn't reach their ends.
Inputs may be any that keep to these rules, and one draw needn't show every extreme that they name: assign holds each of 0 to 127 once. Only the first tile_rank[s, i, j] rank columns of a tile count; some tile has rank exactly 64.
All inputs are finite; a program needn't handle non-finite values.
Results may differ from the reference program's by a relative error of at most 0.0059.
Values may be sent and summed in bfloat16 or wider, within the bound.
A program may use at most 64 MiB of HBM per device.

```python
import math
import jax
import jax.numpy as jnp
from jax import lax

SEISMOGRAM_LEN = 1024
NF = 128
TILE = 128
R = 64
SRC = 1536
VS = 64
RT = 24
RCV = 3072
STILES = 12


def draw_tile_rank(key, part):
    key_wide, key_narrow, key_broad, key_forced = jax.random.split(key, 4)
    wide_slot = jax.random.randint(key_wide, (NF, 1, 1), 0, 4) == 0
    narrow_rank = jax.random.randint(key_narrow, (NF, STILES, RT), 4, R // 2 + 1)
    broad_rank = jax.random.randint(key_broad, (NF, STILES, RT), R // 4, R + 1)
    ranks = jnp.where(wide_slot, broad_rank, narrow_rank)
    forced = jax.random.randint(key_forced, (), 0, NF * STILES * RT)
    ranks = ranks.reshape(-1).at[forced].set(R).reshape(NF, STILES, RT)
    return ranks.astype(jnp.int32)


def raised(values, stream_key, source, target, parts, factor):
    def block_of(axis_at):
        return (jnp.arange(values.shape[axis_at]) // (values.shape[axis_at] // parts)).reshape((-1,) + (1,) * (values.ndim - 1 - axis_at))

    first = jax.random.permutation(stream_key, parts)[block_of(target)]
    other_side = (block_of(target) + parts // 2) % parts
    return jnp.where((block_of(source) == first) | (block_of(source) == other_side), factor * values, values)


def shard_levels(rng, extent, cuts, least, largest):
    loudness, own = 1.0, jax.random.fold_in(rng, 6)
    for position, parts in cuts:
        heights = jnp.exp(jax.random.uniform(jax.random.fold_in(own, position), (parts,), jnp.float32, least / len(cuts), largest / len(cuts)))
        loudness = loudness * jnp.repeat(heights, extent[position] // parts).reshape([-1 if axis == position else 1 for axis in range(len(extent))])
    return loudness


def normal_values(stream_key, shape, scale, reach, pieces=(), kind=jnp.bfloat16):
    array = scale * jax.random.normal(stream_key, shape, jnp.float32)
    if pieces:
        array = array * shard_levels(stream_key, shape, pieces, -0.22, 0.18)
    return jnp.clip(array, -reach, reach).astype(kind)


def noise_with(rng, extent, deviation, most, pieces, heavy, held_as=jnp.bfloat16):
    drawn = deviation * jax.random.normal(rng, extent, jnp.float32)
    if pieces:
        drawn = drawn * shard_levels(rng, extent, pieces, -0.22, 0.18)
    return jnp.clip(raised(drawn, jax.random.fold_in(rng, 3), *heavy), -most, most).astype(held_as)


def setup_inputs(seed: int = 0) -> dict:
    streams_of = jax.random.split(jax.random.key(seed), 6)
    traces = normal_values(streams_of[0], (VS, RCV, SEISMOGRAM_LEN), 1.0, 6.0, ((0, 32), (1, 24)))
    kern_v = normal_values(streams_of[1], (NF, RCV, STILES, 2 * R), (2 * TILE) ** -0.5, 0.375, ((0, 32), (1, 24)))
    kern_u = noise_with(streams_of[2], (NF, RT, SRC, 2 * R), (2 * R * RT) ** -0.5, 0.15625, ((0, 32), (1, 24)), (1, 2, 24, 2.25))
    assign = jax.random.permutation(streams_of[3], NF).astype(jnp.int32)
    tile_rank = draw_tile_rank(jax.random.fold_in(streams_of[5], 71), 0)
    return {"traces": traces, "kern_v": kern_v, "kern_u": kern_u, "assign": assign, "tile_rank": tile_rank}


def spectral_tables(assign):
    spectral_bin_numbers = assign.astype(jnp.int32) + 1
    clock_moments = jnp.arange(SEISMOGRAM_LEN, dtype=jnp.int32)
    rotation_radians = clock_moments[:, None] * spectral_bin_numbers[None, :] % SEISMOGRAM_LEN
    angles = rotation_radians.astype(jnp.float32) * (2.0 * math.pi / SEISMOGRAM_LEN)
    cosine = jnp.cos(angles)
    sine = jnp.sin(angles)
    forward = jnp.concatenate([cosine, -sine], axis=1).astype(jnp.bfloat16)
    inverse_transform = jnp.concatenate([cosine.T, -sine.T], axis=0).astype(jnp.bfloat16)
    return (forward, inverse_transform)

def reference(traces, kern_v, kern_u, assign, tile_rank):
    forward, inverse_transform = spectral_tables(assign)
    spectra = jnp.dot(traces.reshape(VS * RCV, SEISMOGRAM_LEN), forward, preferred_element_type=jnp.float32) * (1.0 / math.sqrt(SEISMOGRAM_LEN))
    spectra = spectra.astype(jnp.bfloat16).reshape(VS, RCV, 2, NF)
    slot_spectra = jnp.moveaxis(spectra, 3, 0)

    def apply_slot(slot_items):
        v_one, u_one, rank_one, x_one = slot_items
        v_tiles = v_one.astype(jnp.float32).reshape(RT, TILE, STILES, 2, R)
        input_tiles = x_one.astype(jnp.float32).reshape(VS, RT, TILE, 2)
        product = jnp.einsum('jtiak,vjtb->jiakbv', v_tiles, input_tiles)
        real_w = product[:, :, 0, :, 0] + product[:, :, 1, :, 1]
        imag_w = product[:, :, 0, :, 1] - product[:, :, 1, :, 0]
        inside = jnp.arange(R, dtype=jnp.int32)[None, None, :, None] < rank_one.T[:, :, None, None]
        real_w = lax.optimization_barrier(jnp.where(inside, real_w, 0.0).astype(jnp.bfloat16)).astype(jnp.float32)
        imag_w = lax.optimization_barrier(jnp.where(inside, imag_w, 0.0).astype(jnp.bfloat16)).astype(jnp.float32)
        u_tiles = u_one.astype(jnp.float32).reshape(RT, STILES, TILE, 2, R)
        u_real = u_tiles[:, :, :, 0]
        u_imag = u_tiles[:, :, :, 1]
        real_y = jnp.einsum('jitk,jikv->itv', u_real, real_w) - jnp.einsum('jitk,jikv->itv', u_imag, imag_w)
        imag_y = jnp.einsum('jitk,jikv->itv', u_real, imag_w) + jnp.einsum('jitk,jikv->itv', u_imag, real_w)
        return jnp.stack([real_y, imag_y], axis=2).reshape(SRC, 2, VS).astype(jnp.bfloat16)
    responses = lax.map(apply_slot, (kern_v, kern_u, tile_rank, slot_spectra))
    flattened = jnp.transpose(responses, (1, 3, 2, 0)).reshape(SRC * VS, 2 * NF)
    result = jnp.dot(flattened, inverse_transform, preferred_element_type=jnp.float32) * (2.0 / math.sqrt(SEISMOGRAM_LEN))
    return result.reshape(SRC, VS, SEISMOGRAM_LEN)
```

```python
import functools
import math

import jax
import jax.numpy as jnp
import ml_dtypes
import numpy as np
from jax import lax
from jax.experimental import pallas as pl
from jax.experimental.pallas import tpu as pltpu
from jax.sharding import PartitionSpec as P

MESH = pl.DeviceIdType.MESH
F32 = jnp.float32
BF16 = jnp.bfloat16
NT = (((1,), (1,)), ((), ()))
NN = (((1,), (0,)), ((), ()))
TN = (((0,), (0,)), ((), ()))


def dot(a, b, dims):
    return lax.dot_general(a, b, dims, preferred_element_type=F32)


def bin_table(bins, moments):
    clock = np.arange(moments)[None, :]
    turns = (np.arange(bins)[:, None] + 1) * clock % moments
    angles = (turns.astype(np.float32) * np.float32(2.0 * math.pi / moments)).astype(np.float64)
    return np.concatenate([np.cos(angles), -np.sin(angles)], axis=0).astype(ml_dtypes.bfloat16)


def shot_order(groups, slots, shots):
    local = shots // groups
    rows = np.arange(groups * 2 * slots)
    lanes = np.arange(slots * 2 * shots)
    group, part, slot = rows // (2 * slots), rows // slots % 2, rows % slots
    lane_slot, lane_part, lane_shot = lanes // (2 * shots), lanes // shots % 2, lanes % shots
    same = (
        (group[:, None] == lane_shot[None, :] // local)
        & (part[:, None] == lane_part[None, :])
        & (slot[:, None] == lane_slot[None, :])
    )
    return same.astype(ml_dtypes.bfloat16)


def kernel(
    nf,
    nr,
    pieces,
    traces_hbm,
    v_hbm,
    u_hbm,
    table_hbm,
    order_hbm,
    assign_ref,
    rank_ref,
    out_ref,
    traces,
    v_raw,
    v_both,
    u_all,
    table,
    order,
    slot_table,
    x_send,
    x_recv,
    x_wide,
    left,
    y_own,
    pair_send,
    pair_recv,
    ring_send,
    ring_recv,
    y_send,
    y_recv,
    load_sem,
    x_sem,
    y_sem,
    pair_send_sem,
    pair_recv_sem,
    ring_send_sem,
    ring_recv_sem,
):
    slots, tiles, rows, cols = v_raw.shape
    half = rows // 2
    rank_cap = cols // 2
    bins = table.shape[0] // 2
    shots = left.shape[1] // 2
    nz = nr // 2
    steps = nz // 2
    wide = slots * cols
    width = wide // pieces
    f = lax.axis_index("freq")
    r = lax.axis_index("rcv")
    z = r // 2
    c = r % 2
    partner = r + 1 - 2 * c
    below = lax.rem(r + nr - 2, nr)
    above = lax.rem(r + 2, nr)

    loads = [
        pltpu.make_async_copy(traces_hbm, traces, load_sem.at[0]),
        pltpu.make_async_copy(table_hbm, table, load_sem.at[1]),
        pltpu.make_async_copy(v_hbm, v_raw, load_sem.at[2]),
        pltpu.make_async_copy(order_hbm, order, load_sem.at[3]),
    ]
    for s in range(slots):
        loads.append(
            pltpu.make_async_copy(u_hbm.at[s], u_all.at[:, pl.ds(s * cols, cols)], load_sem.at[4 + s])
        )
    for load in loads:
        load.start()

    barrier = pltpu.get_barrier_semaphore()

    def greet(i, carry):
        p = lax.rem(f + i, nf)
        pl.semaphore_signal(barrier, inc=1, device_id=(p, r), device_id_type=MESH)
        return carry

    lax.fori_loop(1, nf, greet, 0)
    for other in (partner, below, above):
        pl.semaphore_signal(barrier, inc=1, device_id=(f, other), device_id_type=MESH)

    n2 = 2 * bins
    row = lax.broadcasted_iota(jnp.int32, (n2, bins), 0)
    lane = lax.broadcasted_iota(jnp.int32, (n2, bins), 1)
    slot_of = row // (2 * slots) * slots + row % slots
    held = jnp.where(lane == slot_of, assign_ref[...].astype(F32), 0.0)
    held = jnp.sum(held, axis=1, keepdims=True)
    part_of = lax.broadcasted_iota(jnp.int32, (n2, 1), 0) // slots % 2
    want = held + (part_of * bins).astype(F32)
    lanes = lax.broadcasted_iota(jnp.int32, (n2, n2), 1).astype(F32)
    permute = jnp.where(lanes == want, 1.0, 0.0).astype(BF16)

    loads[0].wait()
    loads[1].wait()
    spectra = dot(table[...], traces[...], NT) * (1.0 / math.sqrt(table.shape[1]))
    spectra = dot(permute, spectra.astype(BF16), NN)
    groups = [spectra[:, k * rows : (k + 1) * rows].reshape(nf, 2 * slots, rows) for k in range(2)]
    block = 4 * slots
    x_send[...] = jnp.concatenate(groups, axis=1).reshape(nf * block, rows).astype(BF16)
    mine = pl.ds(pl.multiple_of(f * block, block), block)
    x_recv[mine, :] = x_send[mine, :]

    pl.semaphore_wait(barrier, nf + 2)

    def send_x(i, carry):
        p = lax.rem(f + i, nf)
        pltpu.make_async_remote_copy(
            src_ref=x_send.at[pl.ds(pl.multiple_of(p * block, block), block), :],
            dst_ref=x_recv.at[mine, :],
            send_sem=x_sem.at[0],
            recv_sem=x_sem.at[1],
            device_id=(p, r),
            device_id_type=MESH,
        ).start()
        return carry

    lax.fori_loop(1, nf, send_x, 0)

    loads[2].wait()
    lane_v = lax.broadcasted_iota(jnp.int32, (rows, cols), 1)
    lane_k = lane_v % rank_cap
    upper = lane_v < rank_cap

    for s in range(slots):

        def prepare(i, carry, s=s):
            v = jnp.where(lane_k < rank_ref[s, i], v_raw[s, i].astype(F32), 0.0)
            turned = pltpu.roll(v, rank_cap, 1)
            v_both[s, i, :rows, :] = v.astype(BF16)
            v_both[s, i, rows:, :] = jnp.where(upper, turned, -turned).astype(BF16)
            return carry

        lax.fori_loop(0, tiles, prepare, 0)
    slot_table[...] = dot(permute, table[...], NN).astype(BF16)
    for load in loads[3:]:
        load.wait()

    all_x = pltpu.make_async_remote_copy(
        src_ref=x_send.at[pl.ds(0, (nf - 1) * block), :],
        dst_ref=x_recv.at[pl.ds(0, (nf - 1) * block), :],
        send_sem=x_sem.at[0],
        recv_sem=x_sem.at[1],
        device_id=(f, partner),
        device_id_type=MESH,
    )
    all_x.wait_recv()
    x_wide[...] = x_recv[...].astype(F32)
    for s in range(slots):
        real = x_wide[pl.ds(s, shots, stride=2 * slots), :].astype(BF16)
        imag = x_wide[pl.ds(slots + s, shots, stride=2 * slots), :].astype(BF16)
        left[s, :shots, :rows] = real
        left[s, :shots, rows:] = imag
        left[s, shots:, :rows] = imag
        left[s, shots:, rows:] = -real

    def tile_at(n):
        if n == 0:
            return lax.rem(z + steps, nz)
        if n == nz - 1:
            return z
        k = (n + 1) // 2
        return lax.rem(z + steps + k, nz) if n % 2 else lax.rem(z + steps + nz - k, nz)

    def pair_copy(n):
        return pltpu.make_async_remote_copy(
            src_ref=pair_send.at[n],
            dst_ref=pair_recv.at[n],
            send_sem=pair_send_sem.at[n],
            recv_sem=pair_recv_sem.at[n],
            device_id=(f, partner),
            device_id_type=MESH,
        )

    def compute(n):
        i = tile_at(n)
        keep = pl.ds(pl.multiple_of(i * rows + c * half, half), half)
        give = pl.ds(pl.multiple_of(i * rows + (1 - c) * half, half), half)
        for s in range(slots):
            w = dot(left[s], v_both[s, i], NN).astype(BF16)
            at = slice(s * cols, (s + 1) * cols)
            u = jnp.concatenate([u_all[keep, at], u_all[give, at]], axis=0)
            y = dot(u, w, NT)
            y_own[n, :, at] = y[:half]
            pair_send[n, :, at] = y[half:].astype(BF16)
        pair_copy(n).start()

    def ring_copy(way, k, p):
        return pltpu.make_async_remote_copy(
            src_ref=ring_send.at[way, k, p],
            dst_ref=ring_recv.at[way, k, p],
            send_sem=ring_send_sem.at[way, k, p],
            recv_sem=ring_recv_sem.at[way, k, p],
            device_id=(f, above if way else below),
            device_id_type=MESH,
        )

    def first_step(way):
        return range(pieces // 2, pieces) if way else range(pieces // 2)

    def ring_step(k):
        for n in (0,) if k == 0 else (2 * k - 1, 2 * k):
            pair_copy(n).wait_recv()
        for p in range(pieces):
            at = slice(p * width, (p + 1) * width)
            for way in range(2):
                if k == 0 and p not in first_step(way):
                    continue
                n = 0 if k == 0 else 2 * k - 1 + way
                total = y_own[n, :, at] + pair_recv[n, :, at].astype(F32)
                if k >= 2 or (k == 1 and p in first_step(way)):
                    ring_copy(way, k - 1, p).wait_recv()
                    total = total + ring_recv[way, k - 1, p].astype(F32)
                ring_send[way, k, p] = total.astype(BF16)
                ring_copy(way, k, p).start()

    compute(0)
    compute(1)
    compute(2)
    for k in range(steps):
        ring_step(k)
        if k + 2 < steps:
            compute(2 * k + 3)
            compute(2 * k + 4)
        elif k + 2 == steps:
            compute(nz - 1)
    n = nz - 1
    pair_copy(n).wait_recv()
    sums = []
    for p in range(pieces):
        at = slice(p * width, (p + 1) * width)
        total = y_own[n, :, at] + pair_recv[n, :, at].astype(F32)
        for way in range(2):
            ring_copy(way, steps - 1, p).wait_recv()
            total = total + ring_recv[way, steps - 1, p].astype(F32)
        sums.append(total)
    response = jnp.concatenate(sums, axis=1)

    even = lax.broadcasted_iota(jnp.int32, (half, wide), 1) % 2 == 0
    stacked = jnp.concatenate(
        [jnp.where(even, response, 0.0).astype(BF16), jnp.where(even, 0.0, response).astype(BF16)], axis=0
    )
    y_send[...] = dot(order[...], stacked, NT)
    eight = 2 * slots
    mine_y = pl.ds(pl.multiple_of(f * eight, eight), eight)
    y_recv[mine_y, :] = y_send[mine_y, :]

    def send_y(i, carry):
        p = lax.rem(f + i, nf)
        pltpu.make_async_remote_copy(
            src_ref=y_send.at[pl.ds(pl.multiple_of(p * eight, eight), eight), :],
            dst_ref=y_recv.at[mine_y, :],
            send_sem=y_sem.at[0],
            recv_sem=y_sem.at[1],
            device_id=(p, r),
            device_id_type=MESH,
        ).start()
        return carry

    lax.fori_loop(1, nf, send_y, 0)
    all_y = pltpu.make_async_remote_copy(
        src_ref=y_send.at[pl.ds(0, (nf - 1) * eight), :],
        dst_ref=y_recv.at[pl.ds(0, (nf - 1) * eight), :],
        send_sem=y_sem.at[0],
        recv_sem=y_sem.at[1],
        device_id=(f, partner),
        device_id_type=MESH,
    )

    all_x.wait_send()
    for n in range(nz):
        pair_copy(n).wait_send()
    for k in range(steps):
        for way in range(2):
            for p in range(pieces):
                if k or p in first_step(way):
                    ring_copy(way, k, p).wait_send()
    all_y.wait_recv()
    result = dot(y_recv[...].astype(BF16), slot_table[...], TN) * (2.0 / math.sqrt(table.shape[1]))
    out_ref[:, 0, :] = result[:half]
    out_ref[:, 1, :] = result[half:]
    all_y.wait_send()


def on_device(nf, nr, traces, kern_v, kern_u, assign, tile_rank):
    local_shots, rows, moments = traces.shape
    slots, _, tiles, cols = kern_v.shape
    sources = kern_u.shape[2]
    bins = assign.shape[0]
    shots = local_shots * nf
    half = rows // 2
    nz = nr // 2
    steps = nz // 2
    pieces = 2
    wide = slots * cols
    table = jnp.asarray(bin_table(bins, moments))
    order = jnp.asarray(shot_order(nf, slots, shots))
    hbm = pl.BlockSpec(memory_space=pl.ANY)
    vmem = pl.BlockSpec(memory_space=pltpu.VMEM)
    return pl.pallas_call(
        functools.partial(kernel, nf, nr, pieces),
        out_shape=jax.ShapeDtypeStruct((half, local_shots, moments), F32),
        in_specs=[hbm] * 5 + [vmem, pl.BlockSpec(memory_space=pltpu.SMEM)],
        out_specs=vmem,
        scratch_shapes=[
            pltpu.VMEM((local_shots * rows, moments), BF16),
            pltpu.VMEM((slots, tiles, rows, cols), BF16),
            pltpu.VMEM((slots, tiles, 2 * rows, cols), BF16),
            pltpu.VMEM((sources, wide), BF16),
            pltpu.VMEM((2 * bins, moments), BF16),
            pltpu.VMEM((nf * 2 * slots, wide), BF16),
            pltpu.VMEM((2 * bins, moments), BF16),
            pltpu.VMEM((nf * 4 * slots, rows), BF16),
            pltpu.VMEM((nf * 4 * slots, rows), BF16),
            pltpu.VMEM((nf * 4 * slots, rows), F32),
            pltpu.VMEM((slots, 2 * shots, 2 * rows), BF16),
            pltpu.VMEM((nz, half, wide), F32),
            pltpu.VMEM((nz, half, wide), BF16),
            pltpu.VMEM((nz, half, wide), BF16),
            pltpu.VMEM((2, steps, pieces, half, wide // pieces), BF16),
            pltpu.VMEM((2, steps, pieces, half, wide // pieces), BF16),
            pltpu.VMEM((nf * 2 * slots, 2 * half), F32),
            pltpu.VMEM((nf * 2 * slots, 2 * half), F32),
            pltpu.SemaphoreType.DMA((4 + slots,)),
            pltpu.SemaphoreType.DMA((2,)),
            pltpu.SemaphoreType.DMA((2,)),
            pltpu.SemaphoreType.DMA((nz,)),
            pltpu.SemaphoreType.DMA((nz,)),
            pltpu.SemaphoreType.DMA((2, steps, pieces)),
            pltpu.SemaphoreType.DMA((2, steps, pieces)),
        ],
        compiler_params=pltpu.CompilerParams(
            collective_id=0, has_side_effects=True, vmem_limit_bytes=48 * 1024 * 1024
        ),
        name="redatum",
    )(
        traces.reshape(local_shots * rows, moments),
        jnp.transpose(kern_v, (0, 2, 1, 3)),
        kern_u.reshape(slots, sources, cols),
        table,
        order,
        assign.reshape(1, bins),
        tile_rank.reshape(slots, tiles),
    )


def solution(mesh):
    placed = (
        P("freq", "rcv", None),
        P("freq", "rcv", None, None),
        P("freq", "rcv", None, None),
        P(),
        P("freq", None, "rcv"),
    )
    return jax.shard_map(
        functools.partial(on_device, mesh.shape["freq"], mesh.shape["rcv"]),
        mesh=mesh,
        in_specs=placed,
        out_specs=P("rcv", "freq", None),
        check_vma=False,
    )
```

```python
import functools
import math

import jax
import jax.numpy as jnp
import ml_dtypes
import numpy as np
from jax import lax
from jax.experimental import pallas as pl
from jax.experimental.pallas import tpu as pltpu
from jax.sharding import PartitionSpec as P

MESH = pl.DeviceIdType.MESH
F32 = jnp.float32
BF16 = jnp.bfloat16
NT = (((1,), (1,)), ((), ()))
NN = (((1,), (0,)), ((), ()))
TN = (((0,), (0,)), ((), ()))
ACROSS = 4


def dot(a, b, dims):
    return lax.dot_general(a, b, dims, preferred_element_type=F32)


def far_first(groups):
    along = groups // ACROSS
    offsets = [(a, b) for a in range(ACROSS) for b in range(along) if (a, b) != (0, 0)]
    return sorted(offsets, key=lambda o: -min(o[0], ACROSS - o[0]) - min(o[1], along - o[1]))


def bin_table(bins, moments):
    clock = np.arange(moments)[None, :]
    turns = (np.arange(bins)[:, None] + 1) * clock % moments
    angles = (turns.astype(np.float32) * np.float32(2.0 * math.pi / moments)).astype(np.float64)
    return np.concatenate([np.cos(angles), -np.sin(angles)], axis=0).astype(ml_dtypes.bfloat16)


def shot_order(groups, slots, shots):
    local = shots // groups
    rows = np.arange(groups * 2 * slots)
    lanes = np.arange(slots * 2 * shots)
    group, part, slot = rows // (2 * slots), rows // slots % 2, rows % slots
    lane_slot, lane_part, lane_shot = lanes // (2 * shots), lanes // shots % 2, lanes % shots
    same = (
        (group[:, None] == lane_shot[None, :] // local)
        & (part[:, None] == lane_part[None, :])
        & (slot[:, None] == lane_slot[None, :])
    )
    return same.astype(ml_dtypes.bfloat16)


def kernel(
    nf,
    nr,
    pieces,
    traces_hbm,
    v_hbm,
    u_hbm,
    table_hbm,
    order_hbm,
    assign_ref,
    rank_ref,
    out_ref,
    traces,
    v_raw,
    v_both,
    u_all,
    table,
    order,
    slot_table,
    x_send,
    x_recv,
    x_wide,
    left,
    y_own,
    pair_send,
    pair_recv,
    ring_send,
    ring_recv,
    y_send,
    y_recv,
    load_sem,
    x_sem,
    y_sem,
    pair_send_sem,
    pair_recv_sem,
    ring_send_sem,
    ring_recv_sem,
):
    slots, tiles, rows, cols = v_raw.shape
    half = rows // 2
    rank_cap = cols // 2
    bins = table.shape[0] // 2
    shots = left.shape[1] // 2
    nz = nr // 2
    steps = nz // 2
    wide = slots * cols
    width = wide // pieces
    f = lax.axis_index("freq")
    r = lax.axis_index("rcv")
    z = r // 2
    c = r % 2
    partner = r + 1 - 2 * c
    mates = [[lax.rem(r + nr - 2 * hops, nr), lax.rem(r + 2 * hops, nr)] for hops in (1, 2)]
    peers = far_first(nf)

    def peer(offset):
        across, along = offset
        columns = nf // ACROSS
        return lax.rem(f // columns + across, ACROSS) * columns + lax.rem(f + along, columns)

    loads = [
        pltpu.make_async_copy(traces_hbm, traces, load_sem.at[0]),
        pltpu.make_async_copy(table_hbm, table, load_sem.at[1]),
        pltpu.make_async_copy(v_hbm, v_raw, load_sem.at[2]),
        pltpu.make_async_copy(order_hbm, order, load_sem.at[3]),
    ]
    for s in range(slots):
        loads.append(
            pltpu.make_async_copy(u_hbm.at[s], u_all.at[:, pl.ds(s * cols, cols)], load_sem.at[4 + s])
        )
    for load in loads:
        load.start()

    barrier = pltpu.get_barrier_semaphore()

    def greet(i, carry):
        p = lax.rem(f + i, nf)
        pl.semaphore_signal(barrier, inc=1, device_id=(p, r), device_id_type=MESH)
        return carry

    lax.fori_loop(1, nf, greet, 0)
    for other in [partner] + mates[0] + mates[1]:
        pl.semaphore_signal(barrier, inc=1, device_id=(f, other), device_id_type=MESH)

    n2 = 2 * bins
    row = lax.broadcasted_iota(jnp.int32, (n2, bins), 0)
    lane = lax.broadcasted_iota(jnp.int32, (n2, bins), 1)
    slot_of = row // (2 * slots) * slots + row % slots
    held = jnp.where(lane == slot_of, assign_ref[...].astype(F32), 0.0)
    held = jnp.sum(held, axis=1, keepdims=True)
    part_of = lax.broadcasted_iota(jnp.int32, (n2, 1), 0) // slots % 2
    want = held + (part_of * bins).astype(F32)
    lanes = lax.broadcasted_iota(jnp.int32, (n2, n2), 1).astype(F32)
    permute = jnp.where(lanes == want, 1.0, 0.0).astype(BF16)

    loads[0].wait()
    loads[1].wait()
    spectra = dot(table[...], traces[...], NT) * (1.0 / math.sqrt(table.shape[1]))
    spectra = dot(permute, spectra.astype(BF16), NN)
    groups = [spectra[:, k * rows : (k + 1) * rows].reshape(nf, 2 * slots, rows) for k in range(2)]
    block = 4 * slots
    x_send[...] = jnp.concatenate(groups, axis=1).reshape(nf * block, rows).astype(BF16)
    mine = pl.ds(pl.multiple_of(f * block, block), block)
    x_recv[mine, :] = x_send[mine, :]

    pl.semaphore_wait(barrier, nf + 4)

    for offset in peers:
        p = peer(offset)
        pltpu.make_async_remote_copy(
            src_ref=x_send.at[pl.ds(pl.multiple_of(p * block, block), block), :],
            dst_ref=x_recv.at[mine, :],
            send_sem=x_sem.at[0],
            recv_sem=x_sem.at[1],
            device_id=(p, r),
            device_id_type=MESH,
        ).start()

    loads[2].wait()
    lane_v = lax.broadcasted_iota(jnp.int32, (rows, cols), 1)
    lane_k = lane_v % rank_cap
    upper = lane_v < rank_cap

    for s in range(slots):

        def prepare(i, carry, s=s):
            v = jnp.where(lane_k < rank_ref[s, i], v_raw[s, i].astype(F32), 0.0)
            turned = pltpu.roll(v, rank_cap, 1)
            v_both[s, i, :rows, :] = v.astype(BF16)
            v_both[s, i, rows:, :] = jnp.where(upper, turned, -turned).astype(BF16)
            return carry

        lax.fori_loop(0, tiles, prepare, 0)
    slot_table[...] = dot(permute, table[...], NN).astype(BF16)
    for load in loads[3:]:
        load.wait()

    all_x = pltpu.make_async_remote_copy(
        src_ref=x_send.at[pl.ds(0, (nf - 1) * block), :],
        dst_ref=x_recv.at[pl.ds(0, (nf - 1) * block), :],
        send_sem=x_sem.at[0],
        recv_sem=x_sem.at[1],
        device_id=(f, partner),
        device_id_type=MESH,
    )
    all_x.wait_recv()
    x_wide[...] = x_recv[...].astype(F32)
    for s in range(slots):
        real = x_wide[pl.ds(s, shots, stride=2 * slots), :].astype(BF16)
        imag = x_wide[pl.ds(slots + s, shots, stride=2 * slots), :].astype(BF16)
        left[s, :shots, :rows] = real
        left[s, :shots, rows:] = imag
        left[s, shots:, :rows] = imag
        left[s, shots:, rows:] = -real

    def tile_at(n):
        if n == 0:
            return lax.rem(z + steps, nz)
        if n == nz - 1:
            return z
        k = (n + 1) // 2
        return lax.rem(z + steps + k, nz) if n % 2 else lax.rem(z + steps + nz - k, nz)

    def pair_copy(n):
        return pltpu.make_async_remote_copy(
            src_ref=pair_send.at[n],
            dst_ref=pair_recv.at[n],
            send_sem=pair_send_sem.at[n],
            recv_sem=pair_recv_sem.at[n],
            device_id=(f, partner),
            device_id_type=MESH,
        )

    def compute(n):
        i = tile_at(n)
        keep = pl.ds(pl.multiple_of(i * rows + c * half, half), half)
        give = pl.ds(pl.multiple_of(i * rows + (1 - c) * half, half), half)
        for s in range(slots):
            w = dot(left[s], v_both[s, i], NN).astype(BF16)
            at = slice(s * cols, (s + 1) * cols)
            u = jnp.concatenate([u_all[keep, at], u_all[give, at]], axis=0)
            y = dot(u, w, NT)
            y_own[n, :, at] = y[:half]
            pair_send[n, :, at] = y[half:].astype(BF16)
        pair_copy(n).start()

    def ring_copy(way, m, p):
        return pltpu.make_async_remote_copy(
            src_ref=ring_send.at[way, m, p],
            dst_ref=ring_recv.at[way, m, p],
            send_sem=ring_send_sem.at[way, m, p],
            recv_sem=ring_recv_sem.at[way, m, p],
            device_id=(f, mates[1 - m % 2][way]),
            device_id_type=MESH,
        )

    def sent(way, m):
        if m:
            return range(pieces)
        return range(pieces // 2, pieces) if way else range(pieces // 2)

    def own_part(n, p):
        at = slice(p * width, (p + 1) * width)
        return y_own[n, :, at] + pair_recv[n, :, at].astype(F32)

    def arrived(way, m, p):
        ring_copy(way, m, p).wait_recv()
        return ring_recv[way, m, p].astype(F32)

    def ring_stage(m):
        for n in (0,) if m == 0 else (2 * m - 1, 2 * m):
            pair_copy(n).wait_recv()
        for p in range(pieces):
            for way in range(2):
                if p not in sent(way, m):
                    continue
                total = own_part(0 if m == 0 else 2 * m - 1 + way, p)
                if m and m % 2 == 0:
                    for before in (m - 2, m - 1):
                        if p in sent(way, before):
                            total = total + arrived(way, before, p)
                ring_send[way, m, p] = total.astype(BF16)
                ring_copy(way, m, p).start()

    compute(0)
    compute(1)
    compute(2)
    ring_stage(0)
    ring_stage(1)
    compute(3)
    compute(4)
    for m in range(2, steps, 2):
        compute(2 * m + 1)
        compute(2 * m + 2)
        ring_stage(m + 1)
        if m + 2 < steps:
            compute(2 * m + 3)
            compute(2 * m + 4)
        else:
            compute(nz - 1)
        ring_stage(m)
    n = nz - 1
    pair_copy(n).wait_recv()
    sums = []
    for p in range(pieces):
        total = own_part(n, p)
        for way in range(2):
            for m in (steps - 2, steps - 1):
                total = total + arrived(way, m, p)
        sums.append(total)
    response = jnp.concatenate(sums, axis=1)

    even = lax.broadcasted_iota(jnp.int32, (half, wide), 1) % 2 == 0
    stacked = jnp.concatenate(
        [jnp.where(even, response, 0.0).astype(BF16), jnp.where(even, 0.0, response).astype(BF16)], axis=0
    )
    y_send[...] = dot(order[...], stacked, NT)
    eight = 2 * slots
    mine_y = pl.ds(pl.multiple_of(f * eight, eight), eight)
    y_recv[mine_y, :] = y_send[mine_y, :]

    for offset in peers:
        p = peer(offset)
        pltpu.make_async_remote_copy(
            src_ref=y_send.at[pl.ds(pl.multiple_of(p * eight, eight), eight), :],
            dst_ref=y_recv.at[mine_y, :],
            send_sem=y_sem.at[0],
            recv_sem=y_sem.at[1],
            device_id=(p, r),
            device_id_type=MESH,
        ).start()

    all_y = pltpu.make_async_remote_copy(
        src_ref=y_send.at[pl.ds(0, (nf - 1) * eight), :],
        dst_ref=y_recv.at[pl.ds(0, (nf - 1) * eight), :],
        send_sem=y_sem.at[0],
        recv_sem=y_sem.at[1],
        device_id=(f, partner),
        device_id_type=MESH,
    )

    all_x.wait_send()
    for n in range(nz):
        pair_copy(n).wait_send()
    for k in range(steps):
        for way in range(2):
            for p in range(pieces):
                if p in sent(way, k):
                    ring_copy(way, k, p).wait_send()
    all_y.wait_recv()
    result = dot(y_recv[...].astype(BF16), slot_table[...], TN) * (2.0 / math.sqrt(table.shape[1]))
    out_ref[:, 0, :] = result[:half]
    out_ref[:, 1, :] = result[half:]
    all_y.wait_send()


def on_device(nf, nr, traces, kern_v, kern_u, assign, tile_rank):
    local_shots, rows, moments = traces.shape
    slots, _, tiles, cols = kern_v.shape
    sources = kern_u.shape[2]
    bins = assign.shape[0]
    shots = local_shots * nf
    half = rows // 2
    nz = nr // 2
    steps = nz // 2
    pieces = 2
    wide = slots * cols
    table = jnp.asarray(bin_table(bins, moments))
    order = jnp.asarray(shot_order(nf, slots, shots))
    hbm = pl.BlockSpec(memory_space=pltpu.HBM)
    vmem = pl.BlockSpec(memory_space=pltpu.VMEM)
    return pl.pallas_call(
        functools.partial(kernel, nf, nr, pieces),
        out_shape=jax.ShapeDtypeStruct((half, local_shots, moments), F32),
        in_specs=[hbm] * 5 + [vmem, pl.BlockSpec(memory_space=pltpu.SMEM)],
        out_specs=vmem,
        scratch_shapes=[
            pltpu.VMEM((local_shots * rows, moments), BF16),
            pltpu.VMEM((slots, tiles, rows, cols), BF16),
            pltpu.VMEM((slots, tiles, 2 * rows, cols), BF16),
            pltpu.VMEM((sources, wide), BF16),
            pltpu.VMEM((2 * bins, moments), BF16),
            pltpu.VMEM((nf * 2 * slots, wide), BF16),
            pltpu.VMEM((2 * bins, moments), BF16),
            pltpu.VMEM((nf * 4 * slots, rows), BF16),
            pltpu.VMEM((nf * 4 * slots, rows), BF16),
            pltpu.VMEM((nf * 4 * slots, rows), F32),
            pltpu.VMEM((slots, 2 * shots, 2 * rows), BF16),
            pltpu.VMEM((nz, half, wide), F32),
            pltpu.VMEM((nz, half, wide), BF16),
            pltpu.VMEM((nz, half, wide), BF16),
            pltpu.VMEM((2, steps, pieces, half, wide // pieces), BF16),
            pltpu.VMEM((2, steps, pieces, half, wide // pieces), BF16),
            pltpu.VMEM((nf * 2 * slots, 2 * half), F32),
            pltpu.VMEM((nf * 2 * slots, 2 * half), F32),
            pltpu.SemaphoreType.DMA((4 + slots,)),
            pltpu.SemaphoreType.DMA((2,)),
            pltpu.SemaphoreType.DMA((2,)),
            pltpu.SemaphoreType.DMA((nz,)),
            pltpu.SemaphoreType.DMA((nz,)),
            pltpu.SemaphoreType.DMA((2, steps, pieces)),
            pltpu.SemaphoreType.DMA((2, steps, pieces)),
        ],
        compiler_params=pltpu.CompilerParams(
            collective_id=0, has_side_effects=True, vmem_limit_bytes=56 * 1024 * 1024
        ),
        name="redatum",
    )(
        traces.reshape(local_shots * rows, moments),
        jnp.transpose(kern_v, (0, 2, 1, 3)),
        kern_u.reshape(slots, sources, cols),
        table,
        order,
        assign.reshape(1, bins),
        tile_rank.reshape(slots, tiles),
    )


def solution(mesh):
    placed = (
        P("freq", "rcv", None),
        P("freq", "rcv", None, None),
        P("freq", "rcv", None, None),
        P(),
        P("freq", None, "rcv"),
    )
    return jax.shard_map(
        functools.partial(on_device, mesh.shape["freq"], mesh.shape["rcv"]),
        mesh=mesh,
        in_specs=placed,
        out_specs=P("rcv", "freq", None),
        check_vma=False,
    )
```

```python
import functools
import math

import jax
import jax.numpy as jnp
import ml_dtypes
import numpy as np
from jax import lax
from jax.experimental import pallas as pl
from jax.experimental.pallas import tpu as pltpu
from jax.sharding import PartitionSpec as P

MESH = pl.DeviceIdType.MESH
F32 = jnp.float32
BF16 = jnp.bfloat16
NT = (((1,), (1,)), ((), ()))
NN = (((1,), (0,)), ((), ()))
TN = (((0,), (0,)), ((), ()))
ACROSS = 4
STRIDE = 2


def dot(a, b, dims):
    return lax.dot_general(a, b, dims, preferred_element_type=F32)


def far_first(groups):
    along = groups // ACROSS
    offsets = [(a, b) for a in range(ACROSS) for b in range(along) if (a, b) != (0, 0)]
    return sorted(offsets, key=lambda o: -min(o[0], ACROSS - o[0]) - min(o[1], along - o[1]))


def bin_table(bins, moments):
    clock = np.arange(moments)[None, :]
    turns = (np.arange(bins)[:, None] + 1) * clock % moments
    angles = (turns.astype(np.float32) * np.float32(2.0 * math.pi / moments)).astype(np.float64)
    return np.concatenate([np.cos(angles), -np.sin(angles)], axis=0).astype(ml_dtypes.bfloat16)


def shot_order(groups, slots, shots):
    local = shots // groups
    rows = np.arange(groups * 2 * slots)
    lanes = np.arange(slots * 2 * shots)
    group, part, slot = rows // (2 * slots), rows // slots % 2, rows % slots
    lane_slot, lane_part, lane_shot = lanes // (2 * shots), lanes // shots % 2, lanes % shots
    same = (
        (group[:, None] == lane_shot[None, :] // local)
        & (part[:, None] == lane_part[None, :])
        & (slot[:, None] == lane_slot[None, :])
    )
    return same.astype(ml_dtypes.bfloat16)


def kernel(
    nf,
    nr,
    pieces,
    traces_hbm,
    v_hbm,
    u_hbm,
    table_hbm,
    order_hbm,
    assign_ref,
    rank_ref,
    out_ref,
    traces,
    v_raw,
    v_both,
    u_all,
    table,
    order,
    slot_table,
    x_send,
    x_recv,
    x_wide,
    left,
    y_own,
    pair_send,
    pair_recv,
    ring_send,
    ring_recv,
    y_send,
    y_recv,
    first_sem,
    load_sem,
    x_sem,
    y_sem,
    pair_send_sem,
    pair_recv_sem,
    ring_send_sem,
    ring_recv_sem,
):
    slots, tiles, rows, cols = v_raw.shape
    half = rows // 2
    rank_cap = cols // 2
    bins = table.shape[0] // 2
    shots = left.shape[1] // 2
    nz = nr // 2
    steps = nz // 2
    wide = slots * cols
    width = wide // pieces
    f = lax.axis_index("freq")
    r = lax.axis_index("rcv")
    z = r // 2
    c = r % 2
    partner = r + 1 - 2 * c
    mates = [[lax.rem(r + nr - 2 * hops, nr), lax.rem(r + 2 * hops, nr)] for hops in range(1, STRIDE + 1)]
    peers = far_first(nf)

    def peer(offset):
        across, along = offset
        columns = nf // ACROSS
        return lax.rem(f // columns + across, ACROSS) * columns + lax.rem(f + along, columns)

    barrier = pltpu.get_barrier_semaphore()
    for offset in peers:
        pl.semaphore_signal(barrier, inc=1, device_id=(peer(offset), r), device_id_type=MESH)
    for other in sum(mates[::-1], []) + [partner]:
        pl.semaphore_signal(barrier, inc=1, device_id=(f, other), device_id_type=MESH)

    parts = 4
    deep = table.shape[1] // parts
    first = []
    for k in range(parts):
        at = pl.ds(k * deep, deep)
        for n, (far, near) in enumerate(((traces_hbm, traces), (table_hbm, table))):
            first.append(pltpu.make_async_copy(far.at[:, at], near.at[:, at], first_sem.at[2 * k + n]))
    for load in first:
        load.start()
    loads = [
        pltpu.make_async_copy(v_hbm, v_raw, load_sem.at[0]),
        pltpu.make_async_copy(order_hbm, order, load_sem.at[1]),
    ]
    for s in range(slots):
        loads.append(
            pltpu.make_async_copy(u_hbm.at[s], u_all.at[:, pl.ds(s * cols, cols)], load_sem.at[2 + s])
        )

    n2 = 2 * bins
    row = lax.broadcasted_iota(jnp.int32, (n2, bins), 0)
    lane = lax.broadcasted_iota(jnp.int32, (n2, bins), 1)
    slot_of = row // (2 * slots) * slots + row % slots
    held = jnp.where(lane == slot_of, assign_ref[...].astype(F32), 0.0)
    held = jnp.sum(held, axis=1, keepdims=True)
    part_of = lax.broadcasted_iota(jnp.int32, (n2, 1), 0) // slots % 2
    want = held + (part_of * bins).astype(F32)
    lanes = lax.broadcasted_iota(jnp.int32, (n2, n2), 1).astype(F32)
    permute = jnp.where(lanes == want, 1.0, 0.0).astype(BF16)

    spectra = jnp.zeros((n2, traces.shape[0]), F32)
    for k in range(parts):
        first[2 * k].wait()
        first[2 * k + 1].wait()
        at = slice(k * deep, (k + 1) * deep)
        spectra = spectra + dot(table[:, at], traces[:, at], NT)
    for load in loads:
        load.start()
    spectra = spectra * (1.0 / math.sqrt(table.shape[1]))
    spectra = dot(permute, spectra.astype(BF16), NN)
    groups = [spectra[:, k * rows : (k + 1) * rows].reshape(nf, 2 * slots, rows) for k in range(2)]
    block = 4 * slots
    x_send[...] = jnp.concatenate(groups, axis=1).reshape(nf * block, rows).astype(BF16)
    mine = pl.ds(pl.multiple_of(f * block, block), block)
    x_recv[mine, :] = x_send[mine, :]

    pl.semaphore_wait(barrier, nf + 2 * STRIDE)

    for offset in peers:
        p = peer(offset)
        pltpu.make_async_remote_copy(
            src_ref=x_send.at[pl.ds(pl.multiple_of(p * block, block), block), :],
            dst_ref=x_recv.at[mine, :],
            send_sem=x_sem.at[0],
            recv_sem=x_sem.at[1],
            device_id=(p, r),
            device_id_type=MESH,
        ).start()

    loads[0].wait()
    lane_v = lax.broadcasted_iota(jnp.int32, (rows, cols), 1)
    lane_k = lane_v % rank_cap
    upper = lane_v < rank_cap

    for s in range(slots):

        def prepare(g, carry, s=s):
            down = lax.rem(z + steps + g, nz)
            up = lax.rem(z + steps + nz - g + steps * ((steps - g) // steps), nz)
            for h, i in enumerate((down, up)):
                v = jnp.where(lane_k < rank_ref[s, i], v_raw[s, i].astype(F32), 0.0)
                turned = pltpu.roll(v, rank_cap, 1)
                at = slice(h * cols, (h + 1) * cols)
                v_both[s, g, :rows, at] = v.astype(BF16)
                v_both[s, g, rows:, at] = jnp.where(upper, turned, -turned).astype(BF16)
            return carry

        lax.fori_loop(0, steps, prepare, 0)
    slot_table[...] = dot(permute, table[...], NN).astype(BF16)
    for load in loads[1:]:
        load.wait()

    all_x = pltpu.make_async_remote_copy(
        src_ref=x_send.at[pl.ds(0, (nf - 1) * block), :],
        dst_ref=x_recv.at[pl.ds(0, (nf - 1) * block), :],
        send_sem=x_sem.at[0],
        recv_sem=x_sem.at[1],
        device_id=(f, partner),
        device_id_type=MESH,
    )
    all_x.wait_recv()
    x_wide[...] = x_recv[...].astype(F32)
    for s in range(slots):
        real = x_wide[pl.ds(s, shots, stride=2 * slots), :].astype(BF16)
        imag = x_wide[pl.ds(slots + s, shots, stride=2 * slots), :].astype(BF16)
        left[s, :shots, :rows] = real
        left[s, :shots, rows:] = imag
        left[s, shots:, :rows] = imag
        left[s, shots:, rows:] = -real

    def tile_at(n):
        if n == 0:
            return lax.rem(z + steps, nz)
        if n == nz - 1:
            return z
        k = (n + 1) // 2
        return lax.rem(z + steps + k, nz) if n % 2 else lax.rem(z + steps + nz - k, nz)

    def pair_copy(n):
        return pltpu.make_async_remote_copy(
            src_ref=pair_send.at[n],
            dst_ref=pair_recv.at[n],
            send_sem=pair_send_sem.at[n],
            recv_sem=pair_recv_sem.at[n],
            device_id=(f, partner),
            device_id_type=MESH,
        )

    def compute(*some):
        for s in range(slots):
            at = slice(s * cols, (s + 1) * cols)
            group = (some[0] + 1) // 2 % steps
            if len(some) == 2:
                both = dot(left[s], v_both[s, group], NN).astype(BF16)
                weights = [both[:, :cols], both[:, cols:]]
            else:
                column = cols if some[0] else 0
                weights = [dot(left[s], v_both[s, group, :, column : column + cols], NN).astype(BF16)]
            for n, w in zip(some, weights):
                i = tile_at(n)
                keep = pl.ds(pl.multiple_of(i * rows + c * half, half), half)
                give = pl.ds(pl.multiple_of(i * rows + (1 - c) * half, half), half)
                u = jnp.concatenate([u_all[keep, at], u_all[give, at]], axis=0)
                y = dot(u, w, NT)
                y_own[n, :, at] = y[:half]
                pair_send[n, :, at] = y[half:].astype(BF16)
        for n in some:
            pair_copy(n).start()

    def ring_copy(way, m, p):
        return pltpu.make_async_remote_copy(
            src_ref=ring_send.at[way, m, p],
            dst_ref=ring_recv.at[way, m, p],
            send_sem=ring_send_sem.at[way, m, p],
            recv_sem=ring_recv_sem.at[way, m, p],
            device_id=(f, mates[(steps - m - 1) % STRIDE][way]),
            device_id_type=MESH,
        )

    def sent(way, m):
        if m:
            return range(pieces)
        return range(pieces // 2, pieces) if way else range(pieces // 2)

    def adds(m):
        return m > 0 and (steps - m) % STRIDE == 0

    def own_part(n, p):
        at = slice(p * width, (p + 1) * width)
        return y_own[n, :, at] + pair_recv[n, :, at].astype(F32)

    def arrived(way, m, p):
        ring_copy(way, m, p).wait_recv()
        return ring_recv[way, m, p].astype(F32)

    def ring_stage(m):
        for n in (0,) if m == 0 else (2 * m - 1, 2 * m):
            pair_copy(n).wait_recv()
        for p in range(pieces):
            for way in range(2):
                if p not in sent(way, m):
                    continue
                total = own_part(0 if m == 0 else 2 * m - 1 + way, p)
                if adds(m):
                    for before in range(m - STRIDE, m):
                        if p in sent(way, before):
                            total = total + arrived(way, before, p)
                ring_send[way, m, p] = total.astype(BF16)
                ring_copy(way, m, p).start()

    compute(0)
    for m in range(1, steps + 1):
        if m < steps:
            compute(2 * m - 1, 2 * m)
        else:
            compute(nz - 1)
        if not adds(m - 1):
            ring_stage(m - 1)
    for m in range(steps):
        if adds(m):
            ring_stage(m)
    n = nz - 1
    pair_copy(n).wait_recv()
    sums = []
    for p in range(pieces):
        total = own_part(n, p)
        for way in range(2):
            for m in range(steps - STRIDE, steps):
                total = total + arrived(way, m, p)
        sums.append(total)
    response = jnp.concatenate(sums, axis=1)

    even = lax.broadcasted_iota(jnp.int32, (half, wide), 1) % 2 == 0
    stacked = jnp.concatenate(
        [jnp.where(even, response, 0.0).astype(BF16), jnp.where(even, 0.0, response).astype(BF16)], axis=0
    )
    y_send[...] = dot(order[...], stacked, NT)
    eight = 2 * slots
    mine_y = pl.ds(pl.multiple_of(f * eight, eight), eight)
    y_recv[mine_y, :] = y_send[mine_y, :]

    for offset in peers:
        p = peer(offset)
        pltpu.make_async_remote_copy(
            src_ref=y_send.at[pl.ds(pl.multiple_of(p * eight, eight), eight), :],
            dst_ref=y_recv.at[mine_y, :],
            send_sem=y_sem.at[0],
            recv_sem=y_sem.at[1],
            device_id=(p, r),
            device_id_type=MESH,
        ).start()

    all_y = pltpu.make_async_remote_copy(
        src_ref=y_send.at[pl.ds(0, (nf - 1) * eight), :],
        dst_ref=y_recv.at[pl.ds(0, (nf - 1) * eight), :],
        send_sem=y_sem.at[0],
        recv_sem=y_sem.at[1],
        device_id=(f, partner),
        device_id_type=MESH,
    )

    all_x.wait_send()
    for n in range(nz):
        pair_copy(n).wait_send()
    for k in range(steps):
        for way in range(2):
            for p in range(pieces):
                if p in sent(way, k):
                    ring_copy(way, k, p).wait_send()
    all_y.wait_recv()
    result = dot(y_recv[...].astype(BF16), slot_table[...], TN) * (2.0 / math.sqrt(table.shape[1]))
    out_ref[:, 0, :] = result[:half]
    out_ref[:, 1, :] = result[half:]
    all_y.wait_send()


def on_device(nf, nr, traces, kern_v, kern_u, assign, tile_rank):
    local_shots, rows, moments = traces.shape
    slots, _, tiles, cols = kern_v.shape
    sources = kern_u.shape[2]
    bins = assign.shape[0]
    shots = local_shots * nf
    half = rows // 2
    nz = nr // 2
    steps = nz // 2
    pieces = 2
    wide = slots * cols
    table = jnp.asarray(bin_table(bins, moments))
    order = jnp.asarray(shot_order(nf, slots, shots))
    hbm = pl.BlockSpec(memory_space=pltpu.HBM)
    vmem = pl.BlockSpec(memory_space=pltpu.VMEM)
    return pl.pallas_call(
        functools.partial(kernel, nf, nr, pieces),
        out_shape=jax.ShapeDtypeStruct((half, local_shots, moments), F32),
        in_specs=[hbm] * 5 + [vmem, pl.BlockSpec(memory_space=pltpu.SMEM)],
        out_specs=vmem,
        scratch_shapes=[
            pltpu.VMEM((local_shots * rows, moments), BF16),
            pltpu.VMEM((slots, tiles, rows, cols), BF16),
            pltpu.VMEM((slots, steps, 2 * rows, 2 * cols), BF16),
            pltpu.VMEM((sources, wide), BF16),
            pltpu.VMEM((2 * bins, moments), BF16),
            pltpu.VMEM((nf * 2 * slots, wide), BF16),
            pltpu.VMEM((2 * bins, moments), BF16),
            pltpu.VMEM((nf * 4 * slots, rows), BF16),
            pltpu.VMEM((nf * 4 * slots, rows), BF16),
            pltpu.VMEM((nf * 4 * slots, rows), F32),
            pltpu.VMEM((slots, 2 * shots, 2 * rows), BF16),
            pltpu.VMEM((nz, half, wide), F32),
            pltpu.VMEM((nz, half, wide), BF16),
            pltpu.VMEM((nz, half, wide), BF16),
            pltpu.VMEM((2, steps, pieces, half, wide // pieces), BF16),
            pltpu.VMEM((2, steps, pieces, half, wide // pieces), BF16),
            pltpu.VMEM((nf * 2 * slots, 2 * half), F32),
            pltpu.VMEM((nf * 2 * slots, 2 * half), F32),
            pltpu.SemaphoreType.DMA((8,)),
            pltpu.SemaphoreType.DMA((2 + slots,)),
            pltpu.SemaphoreType.DMA((2,)),
            pltpu.SemaphoreType.DMA((2,)),
            pltpu.SemaphoreType.DMA((nz,)),
            pltpu.SemaphoreType.DMA((nz,)),
            pltpu.SemaphoreType.DMA((2, steps, pieces)),
            pltpu.SemaphoreType.DMA((2, steps, pieces)),
        ],
        compiler_params=pltpu.CompilerParams(
            collective_id=0, has_side_effects=True, vmem_limit_bytes=56 * 1024 * 1024
        ),
        name="redatum",
    )(
        traces.reshape(local_shots * rows, moments),
        jnp.transpose(kern_v, (0, 2, 1, 3)),
        kern_u.reshape(slots, sources, cols),
        table,
        order,
        assign.reshape(1, bins),
        tile_rank.reshape(slots, tiles),
    )


def solution(mesh):
    placed = (
        P("freq", "rcv", None),
        P("freq", "rcv", None, None),
        P("freq", "rcv", None, None),
        P(),
        P("freq", None, "rcv"),
    )
    return jax.shard_map(
        functools.partial(on_device, mesh.shape["freq"], mesh.shape["rcv"]),
        mesh=mesh,
        in_specs=placed,
        out_specs=P("rcv", "freq", None),
        check_vma=False,
    )
```
